256 devices in a mesh: dp: 32 (over y, z), hg: 8 (over x, core).
Axes of the slice: x: 4, y: 4, z: 8, core: 2. Of those that a mesh axis runs over, the one named last changes fastest.
Arguments:
- w_ukv: bfloat16 [512, 32768], P('dp', 'hg'), may hold values from -1 to 1
- w_uq: bfloat16 [1536, 16384], P('dp', 'hg'), may hold values from -1 to 1
- query_latent: bfloat16 [2, 1024, 1536], P(None, 'dp'), may hold values from -6 to 6
- new_latent: bfloat16 [2, 1024, 512], P(None, 'dp'), may hold values from -12 to 12
- latent_cache: bfloat16 [2048, 128, 512], P('dp'), may hold values from -12 to 12
- cache_lengths: int32 [2048], P('dp'), may hold values from 16 to 128, as said below
- owners: int32 [1024, 1], P('dp'), may hold values from 0 to 31; in each aligned block of 32 rows (0 to 31, 32 to 63, ...) at most 2 rows name the same one
Outputs:
- attention_out: bfloat16 [2, 1024, 16384], P(None, 'dp', 'hg')
The draws below stay inside these ranges and needn't reach their ends.
Inputs may be any that keep to these rules, and one draw needn't show every extreme that they name: `owners`: among the 32 requests of one dp rank no owner is named more than 2 times, a bound that some block reaches. `cache_lengths`: some slot holds exactly 128 tokens.
All inputs are finite; a program needn't handle non-finite values.
Results may differ from the reference program's by a relative error of at most 0.008.
Values may be sent and summed in bfloat16 or wider, within the bound.
A program may use at most 128 MiB of HBM per device.

```python
import math
import jax
import jax.numpy as jnp
import numpy as np
from jax import lax

C = 512
HEADS = 128
NOPE = 128
VDIM = 128
QRANK = 1536
REQ_DEV = 32
MAXLEN = 128
STEPS = 2
REQUESTS = 1024
SEND_CAP = 2
SLOTS = 64
TOTAL_SLOTS = 2048
N_DP = 32


def draw_w_ukv(key, part):
    own_key = jax.random.fold_in(key, 3)
    spread = C ** (-0.5)
    values = jax.random.truncated_normal(own_key, -6.0, 6.0, (C, HEADS, NOPE + VDIM), jnp.float32) * spread
    return values.reshape(C, HEADS * (NOPE + VDIM)).astype(jnp.bfloat16)


def draw_w_uq(key, part):
    own_key = jax.random.fold_in(key, 5)
    spread = QRANK ** (-0.5)
    values = jax.random.truncated_normal(own_key, -6.0, 6.0, (QRANK, HEADS, NOPE), jnp.float32) * spread
    return values.reshape(QRANK, HEADS * NOPE).astype(jnp.bfloat16)


def draw_query_latent(key, part):
    own_key = jax.random.fold_in(key, 7)
    values = jax.random.truncated_normal(own_key, -6.0, 6.0, (STEPS, REQUESTS, QRANK), jnp.float32)
    return values.astype(jnp.bfloat16)


def draw_latent_cache(key, part):
    own_key = jax.random.fold_in(key, 9)
    values = jax.random.truncated_normal(own_key, -6.0, 6.0, (TOTAL_SLOTS, MAXLEN, C), jnp.float32) * 2.0
    return values.astype(jnp.bfloat16)


def draw_cache_lengths(key, part):
    key = jax.random.fold_in(key, 11)
    values = jax.random.randint(key, (TOTAL_SLOTS,), MAXLEN // 8, MAXLEN + 1)
    return values.at[0].set(MAXLEN).astype(jnp.int32)


def level_of(key, dims, pieces, least, top_value):
    factor_of = 1.0
    for axis_at, blocks in pieces:
        steps = jax.random.uniform(jax.random.fold_in(jax.random.fold_in(key, 6), axis_at), (blocks,), jnp.float32, least / len(pieces), top_value / len(pieces))
        factor_of = factor_of * jnp.repeat(jnp.exp(steps), dims[axis_at] // blocks).reshape((-1,) + (1,) * (len(dims) - 1 - axis_at))
    return factor_of


def shared_out(rng, own, number, rows, amount, top, most, slope):
    sequence = jax.random.permutation(rng, amount)
    heavy_load, usual = portions_of(amount, rows * top, most, slope, True), portions_of(amount, rows * top, most, slope, False)
    places = jnp.arange(amount)

    def named(lengths, turn):
        used = int((lengths > 0).sum())
        fixed = max(1, used // 4)
        passed = fixed + (places - fixed + turn * (used - fixed)) % max(1, amount - fixed)
        return jnp.zeros((amount,), jnp.int32).at[sequence[jnp.where(places < fixed, places, passed)]].set(jnp.asarray(lengths, jnp.int32))

    lengths = jnp.where(number % 4 == 0, named(heavy_load, number // 4), named(usual, number - number // 4 - 1))
    mixed = jax.random.permutation(jax.random.fold_in(own, 3), amount)
    donor, taker = mixed[0:amount // 2 * 2:2], mixed[1:amount // 2 * 2:2]
    slack = jnp.minimum(lengths[donor] - 1, most - lengths[taker]) // 2
    slack = jnp.where((donor == sequence[0]) | (taker == sequence[0]) | (lengths[taker] == 0), 0, jnp.maximum(slack, 0))
    passed = jax.random.randint(jax.random.fold_in(own, 4), (amount // 2,), 0, 1 << 20) % (slack + 1)
    lengths = lengths.at[donor].add(-passed).at[taker].add(passed)
    labels = jnp.searchsorted(jnp.cumsum(lengths), jnp.arange(rows * top), side="right").astype(jnp.int32)
    listing = labels.reshape(top, rows).T
    listing = listing[jax.random.permutation(jax.random.fold_in(own, 1), rows)]
    turn = jax.random.randint(jax.random.fold_in(own, 2), (rows, 1), 0, top)
    return jnp.take_along_axis(listing, (jnp.arange(top)[None, :] + turn) % top, axis=1)


def portions_of(count, total, bound, skew, full):
    loads = [(1 << 20) // math.isqrt(grade ** skew) + 1 for grade in range(1, count + 1)]
    largest = bound if full else min(bound, max(-(-total // count), total * loads[0] // sum(loads)))
    least = 1 if total - largest >= count - 1 else 0
    given, surplus = [largest] + [least] * (count - 1), total - largest - least * (count - 1)
    while surplus > 0:
        candidates = [i for i in range(1, count) if given[i] < largest] or [i for i in range(1, count) if given[i] < bound]
        whole, left = sum([loads[i] for i in candidates]), surplus
        for i in candidates:
            extra = min(bound - given[i], max(1, left * loads[i] // whole), surplus)
            given[i] = given[i] + extra
            surplus = surplus - extra
    return np.array(given)


def scatter_about(key, shape, scale, bound, shards=(), held_as=jnp.bfloat16):
    values = jax.random.normal(key, shape, jnp.float32) * scale
    if len(shards) > 0:
        values = level_of(key, shape, shards, -0.22, 0.18) * values
    return jnp.clip(values, min=-bound, max=bound).astype(held_as)


def setup_inputs(seed: int = 0) -> dict:
    key_list = jax.random.split(jax.random.key(seed), 8)
    w_ukv = draw_w_ukv(jax.random.fold_in(key_list[7], 71), 0)
    w_uq = draw_w_uq(jax.random.fold_in(key_list[7], 71), 0)
    query_latent = draw_query_latent(jax.random.fold_in(key_list[7], 71), 0)
    new_latent = scatter_about(key_list[3], (STEPS, REQUESTS, C), 2.0, 12.0, ((1, 32),))
    latent_cache = draw_latent_cache(jax.random.fold_in(key_list[7], 71), 0)
    cache_lengths = draw_cache_lengths(jax.random.fold_in(key_list[7], 71), 0)
    owners_keys = jax.random.split(jax.random.fold_in(key_list[6], 1), REQUESTS // REQ_DEV)
    owners_turns = jax.random.permutation(jax.random.fold_in(key_list[6], 3), REQUESTS // REQ_DEV)
    owners = jax.vmap(lambda own, number: shared_out(jax.random.fold_in(key_list[6], 2), own, number, REQ_DEV, N_DP, 1, SEND_CAP, 2))(owners_keys, owners_turns).reshape((REQUESTS, 1))
    return dict(w_ukv=w_ukv, w_uq=w_uq, query_latent=query_latent, new_latent=new_latent, latent_cache=latent_cache, cache_lengths=cache_lengths, owners=owners)


def reference(w_ukv, w_uq, query_latent, new_latent, latent_cache, cache_lengths, owners):
    owner_rank = owners[:, 0]
    grouped = owner_rank.reshape(N_DP, REQ_DEV)
    onehot = (grouped[:, :, None] == jnp.arange(N_DP, dtype=jnp.int32)[None, None, :]).astype(jnp.int32)
    before = jnp.cumsum(onehot, 1) - onehot
    order_rank = jnp.sum(before * onehot, 2).reshape(REQUESTS)
    home_rank = jnp.arange(REQUESTS, dtype=jnp.int32) // REQ_DEV
    slot_index = (owner_rank * SLOTS + home_rank * SEND_CAP + order_rank).astype(jnp.int32)
    request_cache = latent_cache[slot_index].astype(jnp.float32)
    request_length = cache_lengths[slot_index]
    valid_mask = jnp.arange(MAXLEN, dtype=jnp.int32)[None, :] < request_length[:, None]
    fresh_all = new_latent.astype(jnp.float32)
    gathered = w_ukv.reshape(C, HEADS, NOPE + VDIM)
    key_heads = jnp.transpose(gathered[:, :, :NOPE], (1, 0, 2))
    value_heads = jnp.transpose(gathered[:, :, NOPE:], (1, 0, 2))
    query_heads = jnp.transpose(w_uq.reshape(QRANK, HEADS, NOPE), (1, 0, 2))
    score_scale = NOPE ** -0.5

    def one_head(operands):
        query_up, key_up, value_up = operands
        absorbed = jnp.dot(query_up.astype(jnp.float32), key_up.astype(jnp.float32).T).astype(jnp.bfloat16)
        results = []
        for step_index in range(STEPS):
            query_abs = jnp.dot(query_latent[step_index].astype(jnp.float32), absorbed.astype(jnp.float32))
            query_abs = query_abs.astype(jnp.bfloat16).astype(jnp.float32)
            fresh_stack = fresh_all[: step_index + 1].transpose(1, 0, 2)
            cache_scores = jnp.einsum("rc,rtc->rt", query_abs, request_cache) * score_scale
            cache_scores = jnp.where(valid_mask, cache_scores, -1e30)
            fresh_scores = jnp.einsum("rc,rjc->rj", query_abs, fresh_stack) * score_scale
            peak_score = jnp.maximum(jnp.max(cache_scores, 1), jnp.max(fresh_scores, 1))
            cache_exp = jnp.exp(cache_scores - peak_score[:, None])
            fresh_exp = jnp.exp(fresh_scores - peak_score[:, None])
            denominator = jnp.sum(cache_exp, 1) + jnp.sum(fresh_exp, 1)
            cache_weight = (cache_exp / denominator[:, None]).astype(jnp.bfloat16).astype(jnp.float32)
            fresh_weight = (fresh_exp / denominator[:, None]).astype(jnp.bfloat16).astype(jnp.float32)
            mixed_latent = jnp.einsum("rt,rtc->rc", cache_weight, request_cache)
            mixed_latent = mixed_latent + jnp.einsum("rj,rjc->rc", fresh_weight, fresh_stack)
            mixed_latent = mixed_latent.astype(jnp.bfloat16)
            head_out = jnp.dot(mixed_latent.astype(jnp.float32), value_up.astype(jnp.float32))
            results.append(head_out.astype(jnp.bfloat16))
        return jnp.stack(results, 0)

    per_head = lax.map(one_head, (query_heads, key_heads, value_heads))
    return jnp.transpose(per_head, (1, 2, 0, 3)).reshape(STEPS, REQUESTS, HEADS * VDIM)
```

```python
import jax
import jax.numpy as jnp
from jax import lax
from jax.experimental import pallas as pl
from jax.experimental.pallas import tpu as pltpu
from jax.sharding import PartitionSpec as P

C = 512
NOPE = 128
QRANK = 1536
STEPS = 2
NY = 4
NZ = 8
NX = 4
HEADS = 16
SLOTS = 64
MAXLEN = 128
EXT = 144
ROWS = SLOTS * STEPS
COLS = HEADS * NOPE
HALF = COLS // 2
QUARTER = COLS // NY
PAYCOL = 256
MESH = pl.DeviceIdType.MESH
BF = jnp.bfloat16
F32 = jnp.float32


def iota(shape, dim):
    return lax.broadcasted_iota(jnp.int32, shape, dim)


def dot(a, b):
    return jnp.dot(a, b, preferred_element_type=F32)


def kernel(
    owners_ref, len_ref, uq_ref, ukv_ref, ql_ref, nl_ref, cache_ref, out_ref,
    pay, og, xf, wq, uk, kb, vb, ce, qs, qr, qa, mx, ob, rz, rs, ry,
    loc, xz_s, xz_r, xy_s, xy_r, xx_s, xx_r, xc_s, xc_r,
    wy_s, wy_r, wz_s, wz_r, kz_s, kz_r, ky_s, ky_r, vz_s, vz_r, vy_s, vy_r,
    q_s, q_r, oz_s, oz_r, oy_s, oy_r,
):
    dp = lax.axis_index("dp")
    hg = lax.axis_index("hg")
    y, z = dp // NZ, lax.rem(dp, NZ)
    x, c = hg // 2, lax.rem(hg, 2)

    def at_y(d):
        return lax.rem(y + (d + NY), NY)

    def at_z(d):
        return lax.rem(z + (d + NZ), NZ)

    def at_x(d):
        return lax.rem(x + (d + NX), NX)

    def dev_y(d):
        return (at_y(d) * NZ + z, hg)

    def dev_z(d):
        return (y * NZ + at_z(d), hg)

    def dev_x(d):
        return (dp, at_x(d) * 2 + c)

    sibling = (dp, x * 2 + (1 - c))
    sends = []

    def push(src, dst, send_sem, recv_sem, device):
        copy = pltpu.make_async_remote_copy(
            src_ref=src, dst_ref=dst, send_sem=send_sem, recv_sem=recv_sem,
            device_id=device, device_id_type=MESH,
        )
        copy.start()
        sends.append(copy)

    def arrived(dst, send_sem, recv_sem):
        pltpu.make_async_remote_copy(
            src_ref=dst, dst_ref=dst, send_sem=send_sem, recv_sem=recv_sem,
            device_id=sibling, device_id_type=MESH,
        ).wait_recv()

    barrier = pltpu.get_barrier_semaphore()
    peers = [dev_z(d) for d in range(1, NZ)] + [dev_y(d) for d in range(1, NY)]
    peers += [dev_x(d) for d in range(1, NX)] + [sibling]
    for peer in peers:
        pl.semaphore_signal(barrier, inc=1, device_id=peer, device_id_type=MESH)

    @pl.when(hg < 6)
    def _():
        pltpu.make_async_copy(
            ql_ref.at[:, :, pl.ds(pl.multiple_of(hg * PAYCOL, PAYCOL), PAYCOL)], pay, loc.at[0]
        ).start()

    @pl.when(hg >= 6)
    def _():
        pltpu.make_async_copy(
            nl_ref.at[:, :, pl.ds(pl.multiple_of((hg - 6) * PAYCOL, PAYCOL), PAYCOL)], pay, loc.at[0]
        ).start()

    ukv_in = pltpu.make_async_copy(ukv_ref, uk, loc.at[1])
    ukv_in.start()

    def uq_part(d):
        return uq_ref.at[:, pl.ds(pl.multiple_of(at_y(d) * QUARTER, QUARTER), QUARTER)]

    uq_in = pltpu.make_async_copy(uq_part(0), wq.at[y, z], loc.at[2])
    uq_in.start()
    cache_in = pltpu.make_async_copy(cache_ref, ce.at[:, pl.ds(0, MAXLEN), :], loc.at[3])
    cache_in.start()

    n = 2 * 32
    own_col = jnp.concatenate([owners_ref[...], owners_ref[...]], axis=0).astype(F32)
    row_i, col_i = iota((n, n), 0), iota((n, n), 1)
    eye = row_i == col_i
    own_row = jnp.sum(jnp.where(eye, own_col, 0.0), axis=0, keepdims=True)
    earlier = (own_col == own_row) & (col_i < row_i) & ((col_i // 32) == (row_i // 32))
    place = jnp.sum(jnp.where(earlier, 1.0, 0.0), axis=1, keepdims=True)
    dst_col = own_col * 2.0 + place
    dst_row = jnp.sum(jnp.where(eye, dst_col, 0.0), axis=0, keepdims=True)
    r0, c0 = iota((ROWS, n), 0), iota((ROWS, n), 1)
    want = ((lax.rem(r0 // 4, NY) * NZ + r0 // 16) * 2 + lax.rem(r0 // 2, 2)).astype(F32)
    spread = jnp.where((dst_row == want) & (c0 // 32 == lax.rem(r0, 2)), 1.0, 0.0).astype(BF)
    r1, c1 = iota((n, ROWS), 0), iota((n, ROWS), 1)
    collect = jnp.where(
        (dst_col == (c1 // 2).astype(F32)) & (r1 // 32 == lax.rem(c1, 2)), 1.0, 0.0
    ).astype(BF)
    r2, c2 = iota((ROWS, ROWS), 0), iota((ROWS, ROWS), 1)
    swap = jnp.where(
        c2 == lax.rem(r2 // 4, NZ) * 16 + (r2 // 32) * 4 + lax.rem(r2, 4), 1.0, 0.0
    ).astype(BF)
    r3, c3 = iota((256, ROWS), 0), iota((256, ROWS), 1)
    token = lax.rem(r3, 16)
    fresh_pick = jnp.where(
        (c3 == (r3 // 32) * 16 + y * 4 + lax.rem(r3 // 16, 2) * 2 + token) & (token < 2), 1.0, 0.0
    ).astype(BF)

    pltpu.make_async_copy(ql_ref.at[:, :, pl.ds(0, PAYCOL)], pay, loc.at[0]).wait()
    og[...] = dot(spread, pay[...].reshape(n, PAYCOL)).astype(BF)
    ukv_in.wait()
    for h in range(HEADS):
        cols = pl.ds(h * NOPE, NOPE)
        kb[y, z, :, cols] = uk[:, pl.ds(h * 256, 128)]
        vb[y, z, :, cols] = uk[:, pl.ds(h * 256 + 128, 128)]
    my_rows = pl.ds(pl.multiple_of(y * ROWS + z * 16, 16), 16)
    xf[hg, my_rows, :] = og[pl.ds(pl.multiple_of(z * 16, 16), 16), :]

    pl.semaphore_wait(barrier, len(peers))

    for d in range(1, NZ):
        push(
            og.at[pl.ds(pl.multiple_of(at_z(d) * 16, 16), 16), :], xf.at[hg, my_rows, :],
            xz_s.at[d], xz_r.at[d], dev_z(d),
        )
    for d in range(1, NY):
        push(uq_part(d), wq.at[y, z], wy_s.at[d], wy_r.at[d], dev_y(d))

    lo, hi = pl.ds(0, HALF), pl.ds(HALF, HALF)
    full = pl.ds(0, COLS)

    class Gather:
        def __init__(self, buf, z_s, z_r, y_s, y_r):
            self.buf, self.z_s, self.z_r, self.y_s, self.y_r = buf, z_s, z_r, y_s, y_r

        def block(self, dy, dz, cols=full):
            return self.buf.at[at_y(dy), at_z(dz), :, cols]

        def z_send(self, s):
            right = self.block(0, 1 - s, full if s < 4 else lo)
            push(right, right, self.z_s.at[s - 1], self.z_r.at[s - 1], dev_z(1))
            left = self.block(0, s - 1, full if s < 4 else hi)
            push(left, left, self.z_s.at[3 + s], self.z_r.at[3 + s], dev_z(-1))

        def z_wait(self, s):
            arrived(self.block(0, -s, full if s < 4 else lo), self.z_s.at[s - 1], self.z_r.at[s - 1])
            arrived(self.block(0, s, full if s < 4 else hi), self.z_s.at[3 + s], self.z_r.at[3 + s])

        def blocks(self, s):
            return [0] if s == 0 else [4] if s == 4 else [-s, s]

        def y_send(self, s):
            for dz in self.blocks(s):
                block, i = self.block(0, dz), (dz + NZ) % NZ
                push(block, block, self.y_s.at[i, 0], self.y_r.at[i, 0], dev_y(1))
                push(block, block, self.y_s.at[i, 1], self.y_r.at[i, 1], dev_y(-1))

        def y_relay(self, s):
            for dz in self.blocks(s):
                i = (dz + NZ) % NZ
                arrived(self.block(-1, dz), self.y_s.at[i, 0], self.y_r.at[i, 0])
                half = self.block(-1, dz, lo)
                push(half, half, self.y_s.at[i, 2], self.y_r.at[i, 2], dev_y(1))
                arrived(self.block(1, dz), self.y_s.at[i, 1], self.y_r.at[i, 1])
                half = self.block(1, dz, hi)
                push(half, half, self.y_s.at[i, 3], self.y_r.at[i, 3], dev_y(-1))

        def y_done(self, s):
            for dz in self.blocks(s):
                i = (dz + NZ) % NZ
                arrived(self.block(-2, dz, lo), self.y_s.at[i, 2], self.y_r.at[i, 2])
                arrived(self.block(2, dz, hi), self.y_s.at[i, 3], self.y_r.at[i, 3])

    keys = Gather(kb, kz_s, kz_r, ky_s, ky_r)
    values = Gather(vb, vz_s, vz_r, vy_s, vy_r)
    keys.z_send(1)
    keys.y_send(0)

    def xblock(dx, dy, core):
        return xf.at[
            at_x(dx) * 2 + core, pl.ds(pl.multiple_of(at_y(dy) * ROWS, ROWS), ROWS), :
        ]

    def share(dy):
        block = xblock(0, -dy, c)
        for d in range(1, NX):
            push(block, block, xx_s.at[dy, d], xx_r.at[dy, d], dev_x(d))
        push(block, block, xc_s.at[dy, 0], xc_r.at[dy, 0], sibling)

    for d in range(1, NZ):
        rows = pl.ds(pl.multiple_of(y * ROWS + at_z(-d) * 16, 16), 16)
        arrived(xf.at[hg, rows, :], xz_s.at[d], xz_r.at[d])
    for d in range(1, NY):
        push(xblock(0, 0, c), xblock(0, 0, c), xy_s.at[d], xy_r.at[d], dev_y(d))
    share(0)

    def wq_block(dz, part):
        return wq.at[part, at_z(dz)]

    all_y, low_y, high_y = pl.ds(0, NY), pl.ds(0, 2), pl.ds(2, 2)

    def wq_send(s):
        right = wq_block(1 - s, all_y if s < 4 else low_y)
        push(right, right, wz_s.at[s - 1], wz_r.at[s - 1], dev_z(1))
        left = wq_block(s - 1, all_y if s < 4 else high_y)
        push(left, left, wz_s.at[3 + s], wz_r.at[3 + s], dev_z(-1))

    def wq_wait(s):
        arrived(wq_block(-s, all_y if s < 4 else low_y), wz_s.at[s - 1], wz_r.at[s - 1])
        arrived(wq_block(s, all_y if s < 4 else high_y), wz_s.at[3 + s], wz_r.at[3 + s])

    uq_in.wait()
    for d in range(1, NY):
        arrived(wq.at[at_y(-d), z], wy_s.at[d], wy_r.at[d])
    wq_send(1)

    for s in range(1, 5):
        keys.z_wait(s)
        if s < 4:
            keys.z_send(s + 1)
        keys.y_send(s)
        if s == 1:
            for d in range(1, NY):
                arrived(xblock(0, -d, c), xy_s.at[d], xy_r.at[d])
                share(d)
        wq_wait(s)
        if s < 4:
            wq_send(s + 1)
        keys.y_relay(s - 1)
    values.z_send(1)
    values.y_send(0)
    for dy in range(NY):
        for d in range(1, NX):
            block = xblock(-d, -dy, c)
            arrived(block, xx_s.at[dy, d], xx_r.at[dy, d])
            push(block, block, xc_s.at[dy, d], xc_r.at[dy, d], sibling)
    keys.y_relay(4)
    for dy in range(NY):
        for d in range(NX):
            arrived(xblock(-d, -dy, 1 - c), xc_s.at[dy, d], xc_r.at[dy, d])

    total = None
    for p in range(2):
        lhs = jnp.concatenate([xf[3 * p + i] for i in range(3)], axis=1)
        part = dot(lhs, wq[pl.ds(2 * p, 2)].reshape(QRANK // 2, QUARTER))
        total = part if total is None else total + part
    query = total.astype(BF)
    for hy in range(NY):
        sorted_rows = dot(swap, query[hy * ROWS : (hy + 1) * ROWS]).astype(BF)
        for oy in range(NY):
            qs[oy, hy] = sorted_rows[oy * 32 : (oy + 1) * 32]
    for d in range(1, NY):
        push(qs.at[at_y(d)], qr.at[y], q_s.at[d], q_r.at[d], dev_y(d))
    qr[y] = qs[y]

    cache_in.wait()
    for hy in range(NY):
        rows = pl.ds(hy * ROWS, ROWS)
        fresh = jnp.concatenate([dot(fresh_pick, xf[6 + i, rows, :]) for i in range(2)], axis=1)
        ce[pl.ds(hy * 16, 16), pl.ds(MAXLEN, 16), :] = fresh.astype(BF).reshape(16, 16, C)

    for s in range(1, 4):
        values.z_wait(s)
        values.z_send(s + 1)
        values.y_send(s)
        values.y_relay(s - 1)
    for s in range(5):
        keys.y_done(s)
    for d in range(1, NY):
        arrived(qr.at[at_y(-d)], q_s.at[d], q_r.at[d])

    for h in range(HEADS):
        head_q = qr[h // 4, :, :, pl.ds((h % 4) * NOPE, NOPE)].reshape(ROWS, NOPE)
        head_k = kb[:, :, :, pl.ds(h * NOPE, NOPE)].reshape(C, NOPE)
        absorbed = lax.dot_general(
            head_q, head_k, (((1,), (1,)), ((), ())), preferred_element_type=F32
        )
        for l in range(4):
            qa[l, pl.ds(h, ROWS, stride=HEADS), :] = absorbed[:, l * 128 : (l + 1) * 128]

    values.z_wait(4)
    values.y_send(4)
    values.y_relay(3)

    column = iota((32, EXT), 1)
    second = iota((32, EXT), 0) >= HEADS
    new_ok = (column == MAXLEN) | ((column == MAXLEN + 1) & second)

    def attend(g, carry):
        scores, slots = [], []
        for hy in range(NY):
            for k in range(2):
                slot = (hy * NZ + g) * 2 + k
                slots.append(slot)
                rows = pl.ds(pl.multiple_of(slot * 32, 32), 32)
                a = jnp.concatenate([qa[l, rows, :] for l in range(4)], axis=1)
                s = lax.dot_general(
                    a.astype(BF), ce[slot], (((1,), (1,)), ((), ())),
                    preferred_element_type=F32,
                )
                ok = (column < len_ref[slot]) | new_ok
                scores.append(jnp.where(ok, s * (NOPE**-0.5), -1e30))
        s = jnp.concatenate(scores, axis=0)
        e = jnp.exp(s - jnp.max(s, axis=1, keepdims=True))
        w = (e / jnp.sum(e, axis=1, keepdims=True)).astype(BF)
        for i, slot in enumerate(slots):
            rows = pl.ds(pl.multiple_of((g * 8 + i) * 32, 32), 32)
            mixed = dot(w[i * 32 : (i + 1) * 32], ce[slot])
            for l in range(4):
                mx[l, rows, :] = mixed[:, l * 128 : (l + 1) * 128]
        return carry

    lax.fori_loop(0, NZ, attend, 0)

    values.y_relay(4)
    for s in range(5):
        values.y_done(s)

    parts = [lo, hi]
    for p, cols in enumerate(parts):
        for h in range(p * 8, p * 8 + 8):
            mixed = jnp.concatenate(
                [mx[l, pl.ds(h, ROWS, stride=HEADS), :] for l in range(4)], axis=1
            ).astype(BF)
            head_v = vb[:, :, :, pl.ds(h * NOPE, NOPE)].reshape(C, NOPE)
            ob[:, pl.ds(h * NOPE, NOPE)] = dot(mixed, head_v).astype(BF)
        for d in range(1, NZ):
            push(
                ob.at[pl.ds(pl.multiple_of(at_z(d) * 16, 16), 16), cols], rz.at[z, :, cols],
                oz_s.at[p, d], oz_r.at[p, d], dev_z(d),
            )
        rz[z, :, cols] = ob[pl.ds(pl.multiple_of(z * 16, 16), 16), cols]
    for p, cols in enumerate(parts):
        for d in range(1, NZ):
            arrived(rz.at[at_z(-d), :, cols], oz_s.at[p, d], oz_r.at[p, d])
        back = dot(swap, rz[:, :, cols].reshape(ROWS, HALF)).astype(BF)
        rs[:, :, cols] = back.reshape(NY, 32, HALF)
        for d in range(1, NY):
            push(rs.at[at_y(d), :, cols], ry.at[y, :, cols], oy_s.at[p, d], oy_r.at[p, d], dev_y(d))
        ry[y, :, cols] = rs[y, :, cols]
    for p, cols in enumerate(parts):
        for d in range(1, NY):
            arrived(ry.at[at_y(-d), :, cols], oy_s.at[p, d], oy_r.at[p, d])
        home = dot(collect, ry[:, :, cols].reshape(ROWS, HALF)).astype(BF)
        out_ref[:, :, cols] = home.reshape(STEPS, 32, HALF)

    for copy in sends:
        copy.wait_send()


def local(w_ukv, w_uq, query_latent, new_latent, latent_cache, cache_lengths, owners):
    dma = pltpu.SemaphoreType.DMA
    pairs = [(8,), (4,), (4, 4), (4, 4), (4,), (8,), (8,), (8, 4), (8,), (8, 4), (4,), (2, 8), (2, 4)]
    sems = [dma((4,))]
    for shape in pairs:
        sems += [dma(shape), dma(shape)]
    scratch = [
        pltpu.VMEM((2, 32, PAYCOL), BF),
        pltpu.VMEM((ROWS, PAYCOL), BF),
        pltpu.VMEM((8, NY * ROWS, PAYCOL), BF),
        pltpu.VMEM((NY, NZ, 48, QUARTER), BF),
        pltpu.VMEM((16, 2 * COLS), BF),
        pltpu.VMEM((NY, NZ, 16, COLS), BF),
        pltpu.VMEM((NY, NZ, 16, COLS), BF),
        pltpu.VMEM((SLOTS, EXT, C), BF),
        pltpu.VMEM((NY, NY, 32, QUARTER), BF),
        pltpu.VMEM((NY, NY, 32, QUARTER), BF),
        pltpu.VMEM((4, ROWS * HEADS, 128), F32),
        pltpu.VMEM((4, ROWS * HEADS, 128), F32),
        pltpu.VMEM((ROWS, COLS), BF),
        pltpu.VMEM((NZ, 16, COLS), BF),
        pltpu.VMEM((NY, 32, COLS), BF),
        pltpu.VMEM((NY, 32, COLS), BF),
    ]
    return pl.pallas_call(
        kernel,
        out_shape=jax.ShapeDtypeStruct((STEPS, 32, COLS), BF),
        in_specs=[
            pl.BlockSpec(memory_space=pltpu.VMEM),
            pl.BlockSpec(memory_space=pltpu.SMEM),
        ]
        + [pl.BlockSpec(memory_space=pl.ANY)] * 5,
        out_specs=pl.BlockSpec(memory_space=pltpu.VMEM),
        scratch_shapes=scratch + sems,
        compiler_params=pltpu.CompilerParams(
            collective_id=0, has_side_effects=True, vmem_limit_bytes=50 * 1024 * 1024
        ),
    )(owners, cache_lengths, w_uq, w_ukv, query_latent, new_latent, latent_cache)


def solution(mesh):
    in_specs = (
        P("dp", "hg"),
        P("dp", "hg"),
        P(None, "dp", None),
        P(None, "dp", None),
        P("dp", None, None),
        P("dp"),
        P("dp", None),
    )
    out_specs = P(None, "dp", "hg")
    return jax.shard_map(local, mesh=mesh, in_specs=in_specs, out_specs=out_specs, check_vma=False)
```
